512 devices in a mesh: grp: 32 (over y, x, core), rep: 16 (over z).
Axes of the slice: x: 4, y: 4, z: 16, core: 2. Of those that a mesh axis runs over, the one named last changes fastest.
Arguments:
- amplitudes: float32 [2, 112, 512, 512], P(None, None, ('grp', 'rep')), may hold values from -6 to 6
- ladder_ints: bfloat16 [512, 512, 2, 512], P(('grp', 'rep')), may hold values from -0.09375 to 0.09375
- cycle_ints: float32 [112, 512, 112, 2], P(None, ('grp', 'rep')), may hold values from -0.0234375 to 0.0234375
- virt_sym: int32 [512], replicated, may hold values from 0 to 3
Outputs:
- residual: float32 [112, 2, 2, 512], P('rep', None, None, 'grp')
The draws below stay inside these ranges and needn't reach their ends.
All inputs are finite; a program needn't handle non-finite values.
Results may differ from the reference program's by a relative error of at most 0.0003.
Values sent between devices are 32-bit elements; how exact they have to be, the bound alone decides.
No kernel may reach another device: no remote copies, remote signals or barrier semaphores. Data moves between devices by JAX's collectives and lax.ppermute only.
A program may use at most 64 MiB of HBM per device.

```python
import jax
import jax.numpy as jnp
from jax import lax

O = 112
V = 512
NI = 2
SA = 2


def with_ends(array, key, low, largest):
    extent = array.shape
    index_at = [jax.random.randint(jax.random.fold_in(key, axis), (), 0, extent[axis]) for axis in range(len(extent))]
    array = array.at[tuple(index_at)].set(low)
    longest = extent.index(max(extent))
    index_at[longest] = (index_at[longest] + 1) % extent[longest]
    return array.at[tuple(index_at)].set(largest)


def with_spikes(result, stream_key, source, target, parts, factor):
    def block_of(position):
        return (jnp.arange(result.shape[position]) // (result.shape[position] // parts)).reshape((-1,) + (1,) * (result.ndim - 1 - position))

    first = jax.random.permutation(stream_key, parts)[block_of(target)]
    second = (block_of(target) + parts // 2) % parts
    return jnp.where((block_of(source) == first) | (block_of(source) == second), factor * result, result)


def block_scale(rng, extent, shards, least, largest):
    loudness = 1.0
    for position, parts in shards:
        heights = jax.random.uniform(jax.random.fold_in(jax.random.fold_in(rng, 6), position), (parts,), jnp.float32, least / len(shards), largest / len(shards))
        loudness = loudness * jnp.repeat(jnp.exp(heights), extent[position] // parts).reshape((-1,) + (1,) * (len(extent) - 1 - position))
    return loudness


def noise(rng, shape, deviation, reach, cuts=(), kind=jnp.bfloat16):
    entries = jax.random.normal(rng, shape, jnp.float32) * deviation
    if len(cuts) > 0:
        entries = block_scale(rng, shape, cuts, -0.22, 0.18) * entries
    return jnp.clip(entries, min=-reach, max=reach).astype(kind)


def noise_with(own_key, extent, deviation, most, shards, heavy, kind=jnp.bfloat16):
    array = deviation * jax.random.normal(own_key, extent, jnp.float32)
    if shards:
        array = array * block_scale(own_key, extent, shards, -0.22, 0.18)
    return jnp.clip(with_spikes(array, jax.random.fold_in(own_key, 3), *heavy), -most, most).astype(kind)


def setup_inputs(seed: int = 0) -> dict:
    key_of = jax.random.split(jax.random.key(seed), 5)
    return {
        "amplitudes": noise(key_of[0], (NI, O, V, V), 1.0, 6.0, ((2, 512),), jnp.float32),
        "ladder_ints": noise_with(key_of[1], (V, V, SA, V), (V * V // 4) ** -0.5, 0.09375, ((0, 512),), (0, 3, 512, 6.0)),
        "cycle_ints": noise(key_of[2], (O, V, O, SA), (O * V) ** -0.5, 0.0234375, ((1, 512),), jnp.float32),
        "virt_sym": with_ends(jax.random.randint(key_of[3], (V,), 0, 4), jax.random.fold_in(key_of[3], 1), 0, 3).astype(jnp.int32),
    }


def reference(amplitudes, ladder_ints, cycle_ints, virt_sym):
    slab_sym = virt_sym[:SA]

    def add_virtual(running, virtual):
        amp_slice = lax.dynamic_index_in_dim(amplitudes, virtual, 2, keepdims=False)
        ints_slice = lax.dynamic_index_in_dim(ladder_ints, virtual, 0, keepdims=False)
        cycle_slice = lax.dynamic_index_in_dim(cycle_ints, virtual, 1, keepdims=False)
        own_sym = lax.dynamic_index_in_dim(virt_sym, virtual, 0, keepdims=False)
        sym_label = jnp.bitwise_xor(jnp.bitwise_xor(own_sym, virt_sym)[:, None, None], jnp.bitwise_xor(slab_sym[:, None], virt_sym[None, :])[None])
        masked = jnp.where(sym_label == 0, ints_slice.astype(jnp.float32), jnp.zeros(ints_slice.shape, jnp.float32))
        ladder = jnp.dot(amp_slice.reshape(NI * O, V), masked.reshape(V, SA * V), preferred_element_type=jnp.float32, precision=lax.Precision.HIGHEST)
        cycle_term = jnp.einsum("kja,ikb->ijab", cycle_slice.astype(jnp.float32), amp_slice.astype(jnp.float32), precision=lax.Precision.HIGHEST)
        return running + ladder.reshape(NI, O, SA, V) + cycle_term, None

    start = jnp.zeros((NI, O, SA, V), jnp.float32)
    running, unused = lax.scan(add_virtual, start, jnp.arange(V, dtype=jnp.int32))
    return jnp.transpose(running, (1, 0, 2, 3)).astype(jnp.float32)
```

```python
import functools

import jax
import jax.numpy as jnp
from jax import lax
from jax.experimental import pallas as pl
from jax.experimental.pallas import tpu as pltpu
from jax.sharding import PartitionSpec as P

LANES = 128


def halves(value):
    high = value.astype(jnp.bfloat16)
    low = (value - high.astype(jnp.float32)).astype(jnp.bfloat16)
    return high, low


def dot(left, right):
    return jnp.dot(left, right, preferred_element_type=jnp.float32)


def lane_index(rows):
    return lax.broadcasted_iota(jnp.int32, (rows, LANES), 1)


def partial_kernel(owner_of, amps_ref, ints_ref, cycle_ref, sym_ref, sym_scalars, out_ref, wide_ref):
    tiles = 4
    rows = 224
    occupied = 112
    wide_ref[...] = ints_ref[...].astype(jnp.float32)
    own_sym = sym_scalars[owner_of()]
    chunks = [halves(amps_ref[pl.ds(tile, rows, stride=tiles), :]) for tile in range(tiles)]
    left = jnp.concatenate(
        [
            jnp.concatenate([high for high, _ in chunks], axis=1),
            jnp.concatenate([low for _, low in chunks], axis=1),
        ],
        axis=0,
    )
    pad = LANES - occupied
    turned = []
    for a in range(2):
        block = cycle_ref[pl.ds(a, occupied, stride=2), :]
        block = jnp.concatenate([block, jnp.zeros((pad, occupied), jnp.float32)], axis=0)
        block = jnp.concatenate([block, jnp.zeros((LANES, pad), jnp.float32)], axis=1)
        turned.append(block.T[:occupied])
    cycle_high, cycle_low = halves(jnp.concatenate(turned, axis=0))
    cycle_left = jnp.concatenate([cycle_high, cycle_low, cycle_high], axis=1)
    zero_rows = jnp.zeros((pad, 2 * LANES), jnp.bfloat16)
    sym_columns = jnp.concatenate(
        [jnp.broadcast_to(sym_ref[tile : tile + 1, :], (LANES, LANES)).T for tile in range(tiles)], axis=0
    )
    lanes = lane_index(8)
    for tile in range(tiles):
        label = jnp.bitwise_xor(sym_columns, sym_ref[tile : tile + 1, :])
        masked = []
        for a in range(2):
            block = wide_ref[pl.ds(tile * 2 + a, 512, stride=8), :]
            wanted = jnp.bitwise_xor(own_sym, sym_scalars[a])
            masked.append(jnp.where(label == wanted, block, 0.0).astype(jnp.bfloat16))
        both = dot(left, jnp.concatenate(masked, axis=1))
        ladder = both[:rows] + both[rows:]
        high, low = chunks[tile]
        high = jnp.concatenate([high[:occupied], high[occupied:]], axis=1)
        low = jnp.concatenate([low[:occupied], low[occupied:]], axis=1)
        cycle_right = jnp.concatenate([high, zero_rows, high, zero_rows, low, zero_rows], axis=0)
        cycle = dot(cycle_left, cycle_right)
        firsts, seconds = [], []
        for a in range(2):
            total = ladder[:, a * LANES : (a + 1) * LANES] + jnp.concatenate(
                [cycle[a * occupied : (a + 1) * occupied, i * LANES : (i + 1) * LANES] for i in range(2)], axis=0
            )
            firsts.append(total[:LANES].T)
            rest = jnp.concatenate([total[LANES:], jnp.zeros((2 * LANES - rows, LANES), jnp.float32)], axis=0)
            seconds.append(rest.T)
        for part in range(8):
            g = tile * 8 + part
            at = part * 16
            out_ref[g, 0:16, :] = firsts[0][at : at + 16]
            out_ref[g, 16:32, :] = firsts[1][at : at + 16]
            last = seconds[1][at + 8 : at + 16]
            body = [seconds[0][at : at + 8], seconds[0][at + 8 : at + 16], seconds[1][at : at + 8]]
            for piece in range(3):
                moved = pltpu.roll(last, 96 - 32 * piece, 1)
                out_ref[g, 32 + 8 * piece : 40 + 8 * piece, :] = jnp.where(lanes < 96, body[piece], moved)


def middle_kernel(in_ref, out_ref, turned_ref):
    total = in_ref[0]
    for source in range(1, in_ref.shape[0]):
        total = total + in_ref[source]
    lanes = lane_index(8)
    last = jnp.zeros((8, LANES), jnp.float32)
    for piece in range(3):
        moved = pltpu.roll(total[32 + 8 * piece : 40 + 8 * piece], 32 * piece + 32, 1)
        last = jnp.where((lanes >= 32 * piece) & (lanes < 32 * piece + 32), moved, last)
    fill = jnp.zeros((LANES - 32, LANES), jnp.float32)
    turned_ref[0:LANES, :] = jnp.concatenate([total[:32], fill], axis=0).T
    turned_ref[LANES:, :] = jnp.concatenate([total[32:56], last, fill], axis=0).T
    wide = lane_index(16)
    for i in range(2):
        dest = [jnp.zeros((16, LANES), jnp.float32) for _ in range(2)]
        for jj in range(7):
            rows = turned_ref[pl.ds(i * 112 + jj, 16, stride=7), :]
            for a in range(2):
                moved = pltpu.roll(rows, (jj * 16 - a * 16) % LANES, 1)
                dest[a] = jnp.where((wide >= jj * 16) & (wide < jj * 16 + 16), moved, dest[a])
        for a in range(2):
            out_ref[pl.ds(i * 2 + a, 16, stride=4), :] = dest[a]


def last_kernel(in_ref, out_ref):
    total = in_ref[0]
    for source in range(1, in_ref.shape[0]):
        total = total + in_ref[source]
    for jj in range(7):
        for i in range(2):
            out_ref[jj, i] = total[2 * i : 2 * i + 2, jj * 16 : jj * 16 + 16]


def shards(amplitudes, ladder_ints, cycle_ints, virt_sym):
    amps = amplitudes.reshape(896, LANES)
    ints = ladder_ints.reshape(512, 2, 4, LANES).transpose(0, 2, 1, 3).reshape(4096, LANES)
    cycle = cycle_ints.reshape(112, 112, 2).transpose(0, 2, 1).reshape(224, 112)

    def owner_of():
        return lax.axis_index("grp") * 16 + lax.axis_index("rep")

    vmem = pl.BlockSpec(memory_space=pltpu.VMEM)
    smem = pl.BlockSpec(memory_space=pltpu.SMEM)
    partial = pl.pallas_call(
        functools.partial(partial_kernel, owner_of),
        out_shape=jax.ShapeDtypeStruct((32, 56, LANES), jnp.float32),
        in_specs=[vmem, vmem, vmem, vmem, smem],
        out_specs=vmem,
        scratch_shapes=[pltpu.VMEM((4096, LANES), jnp.float32)],
        compiler_params=pltpu.CompilerParams(vmem_limit_bytes=32 * 1024 * 1024),
        name="partial",
    )(amps, ints, cycle, virt_sym.reshape(4, LANES), virt_sym)
    received = lax.all_to_all(partial, "grp", 0, 0, tiled=True)
    middle = pl.pallas_call(
        middle_kernel,
        out_shape=jax.ShapeDtypeStruct((64, LANES), jnp.float32),
        in_specs=[vmem],
        out_specs=vmem,
        scratch_shapes=[pltpu.VMEM((256, LANES), jnp.float32)],
        name="middle",
    )(received)
    received = lax.all_to_all(middle.reshape(16, 4, LANES), "rep", 0, 0, tiled=True)
    return pl.pallas_call(
        last_kernel,
        out_shape=jax.ShapeDtypeStruct((7, 2, 2, 16), jnp.float32),
        in_specs=[vmem],
        out_specs=vmem,
        name="last",
    )(received)


def solution(mesh):
    return jax.shard_map(
        shards,
        mesh=mesh,
        in_specs=(
            P(None, None, ("grp", "rep"), None),
            P(("grp", "rep"), None, None, None),
            P(None, ("grp", "rep"), None, None),
            P(),
        ),
        out_specs=P("rep", None, None, "grp"),
        check_vma=False,
    )
```

```python
import functools

import jax
import jax.numpy as jnp
from jax import lax
from jax.experimental import pallas as pl
from jax.experimental.pallas import tpu as pltpu
from jax.sharding import PartitionSpec as P

LANES = 128


def halves(value):
    high = value.astype(jnp.bfloat16)
    low = (value - high.astype(jnp.float32)).astype(jnp.bfloat16)
    return high, low


def dot(left, right):
    return jnp.dot(left, right, preferred_element_type=jnp.float32)


def lane_index(rows):
    return lax.broadcasted_iota(jnp.int32, (rows, LANES), 1)


def packed(firsts, seconds, at, lanes):
    pieces = [firsts[a][at + half : at + half + 8] for a in range(2) for half in (0, 8)]
    body = [seconds[0][at : at + 8], seconds[0][at + 8 : at + 16], seconds[1][at : at + 8]]
    last = seconds[1][at + 8 : at + 16]
    for piece in range(3):
        moved = pltpu.roll(last, 96 - 32 * piece, 1)
        pieces.append(jnp.where(lanes < 96, body[piece], moved))
    return pieces


def partial_kernel(
    place_of, amps_hbm, ints_hbm, cycle_hbm, sym_hbm, labels_hbm, keep_ref, send_ref,
    amps_ref, ints_ref, cycle_ref, sym_ref, sym_scalars, wide_ref, sems,
):
    tiles = 4
    rows = 224
    occupied = 112
    parts = 4
    depth = 4096 // parts
    pairs = [(labels_hbm, sym_scalars), (sym_hbm, sym_ref), (amps_hbm, amps_ref), (cycle_hbm, cycle_ref)]
    for part in range(parts):
        at = pl.ds(part * depth, depth)
        pairs.append((ints_hbm.at[at], ints_ref.at[at]))
    copies = [pltpu.make_async_copy(source, target, sems.at[n]) for n, (source, target) in enumerate(pairs)]
    for copy in copies:
        copy.start()
    owner, core = place_of()
    for copy in copies[:4]:
        copy.wait()
    own_sym = sym_scalars[owner]
    chunks = [halves(amps_ref[pl.ds(tile, rows, stride=tiles), :]) for tile in range(tiles)]
    left = jnp.concatenate(
        [
            jnp.concatenate([high for high, _ in chunks], axis=1),
            jnp.concatenate([low for _, low in chunks], axis=1),
        ],
        axis=0,
    )
    pad = LANES - occupied
    turned = []
    for a in range(2):
        block = cycle_ref[pl.ds(a, occupied, stride=2), :]
        block = jnp.concatenate([block, jnp.zeros((pad, occupied), jnp.float32)], axis=0)
        block = jnp.concatenate([block, jnp.zeros((LANES, pad), jnp.float32)], axis=1)
        turned.append(block.T[:occupied])
    cycle_high, cycle_low = halves(jnp.concatenate(turned, axis=0))
    cycle_left = jnp.concatenate([cycle_high, cycle_low, cycle_high], axis=1)
    zero_rows = jnp.zeros((pad, 2 * LANES), jnp.bfloat16)
    sym_columns = jnp.concatenate(
        [jnp.broadcast_to(sym_ref[tile : tile + 1, :], (LANES, LANES)).T for tile in range(tiles)], axis=0
    )
    lanes = lane_index(8)
    for part in range(parts):
        copies[4 + part].wait()
        at = pl.ds(part * depth, depth)
        wide_ref[at, :] = ints_ref[at, :].astype(jnp.float32)
    for tile in range(tiles):
        label = jnp.bitwise_xor(sym_columns, sym_ref[tile : tile + 1, :])
        masked = []
        for a in range(2):
            block = wide_ref[pl.ds(tile * 2 + a, 512, stride=8), :]
            wanted = jnp.bitwise_xor(own_sym, sym_scalars[a])
            masked.append(jnp.where(label == wanted, block, 0.0).astype(jnp.bfloat16))
        both = dot(left, jnp.concatenate(masked, axis=1))
        ladder = both[:rows] + both[rows:]
        high, low = chunks[tile]
        high = jnp.concatenate([high[:occupied], high[occupied:]], axis=1)
        low = jnp.concatenate([low[:occupied], low[occupied:]], axis=1)
        cycle_right = jnp.concatenate([high, zero_rows, high, zero_rows, low, zero_rows], axis=0)
        cycle = dot(cycle_left, cycle_right)
        firsts, seconds = [], []
        for a in range(2):
            total = ladder[:, a * LANES : (a + 1) * LANES] + jnp.concatenate(
                [cycle[a * occupied : (a + 1) * occupied, i * LANES : (i + 1) * LANES] for i in range(2)], axis=0
            )
            firsts.append(total[:LANES].T)
            rest = jnp.concatenate([total[LANES:], jnp.zeros((2 * LANES - rows, LANES), jnp.float32)], axis=0)
            seconds.append(rest.T)
        for part in range(4):
            chip = tile * 4 + part
            blocks = [packed(firsts, seconds, part * 32 + 16 * side, lanes) for side in range(2)]
            for at in range(0, 56, 8):
                zero, one = blocks[0][at // 8], blocks[1][at // 8]
                keep_ref[chip, at : at + 8, :] = jnp.where(core == 0, zero, one)
                send_ref[chip, at : at + 8, :] = jnp.where(core == 0, one, zero)


def middle_kernel(in_ref, out_ref, turned_ref):
    total = in_ref[0]
    for source in range(1, in_ref.shape[0]):
        total = total + in_ref[source]
    lanes = lane_index(8)
    last = jnp.zeros((8, LANES), jnp.float32)
    for piece in range(3):
        moved = pltpu.roll(total[32 + 8 * piece : 40 + 8 * piece], 32 * piece + 32, 1)
        last = jnp.where((lanes >= 32 * piece) & (lanes < 32 * piece + 32), moved, last)
    fill = jnp.zeros((LANES - 32, LANES), jnp.float32)
    turned_ref[0:LANES, :] = jnp.concatenate([total[:32], fill], axis=0).T
    turned_ref[LANES:, :] = jnp.concatenate([total[32:56], last, fill], axis=0).T
    wide = lane_index(16)
    for i in range(2):
        dest = [jnp.zeros((16, LANES), jnp.float32) for _ in range(2)]
        for jj in range(7):
            rows = turned_ref[pl.ds(i * 112 + jj, 16, stride=7), :]
            for a in range(2):
                moved = pltpu.roll(rows, (jj * 16 - a * 16) % LANES, 1)
                dest[a] = jnp.where((wide >= jj * 16) & (wide < jj * 16 + 16), moved, dest[a])
        for a in range(2):
            out_ref[pl.ds(i * 2 + a, 16, stride=4), :] = dest[a]


def last_kernel(in_ref, out_ref):
    total = in_ref[0]
    for source in range(1, in_ref.shape[0]):
        total = total + in_ref[source]
    for jj in range(7):
        for i in range(2):
            out_ref[jj, i] = total[2 * i : 2 * i + 2, jj * 16 : jj * 16 + 16]


def shards(amplitudes, ladder_ints, cycle_ints, virt_sym):
    amps = amplitudes.reshape(896, LANES)
    ints = ladder_ints.reshape(512, 2, 4, LANES).transpose(0, 2, 1, 3).reshape(4096, LANES)
    cycle = cycle_ints.reshape(112, 112, 2).transpose(0, 2, 1).reshape(224, 112)

    def place_of():
        group = lax.axis_index("grp")
        return group * 16 + lax.axis_index("rep"), lax.rem(group, 2)

    hbm = pl.BlockSpec(memory_space=pltpu.HBM)
    vmem = pl.BlockSpec(memory_space=pltpu.VMEM)
    operands = (amps, ints, cycle, virt_sym.reshape(4, LANES), virt_sym)
    half = jax.ShapeDtypeStruct((16, 56, LANES), jnp.float32)
    keep, send = pl.pallas_call(
        functools.partial(partial_kernel, place_of),
        out_shape=(half, half),
        in_specs=[hbm] * 5,
        out_specs=(vmem, vmem),
        scratch_shapes=[
            pltpu.VMEM((896, LANES), jnp.float32),
            pltpu.VMEM((4096, LANES), jnp.bfloat16),
            pltpu.VMEM((224, 112), jnp.float32),
            pltpu.VMEM((4, LANES), jnp.int32),
            pltpu.SMEM((512,), jnp.int32),
            pltpu.VMEM((4096, LANES), jnp.float32),
            pltpu.SemaphoreType.DMA((8,)),
        ],
        compiler_params=pltpu.CompilerParams(vmem_limit_bytes=32 * 1024 * 1024),
        name="partial",
    )(*(pltpu.with_memory_space_constraint(array, pltpu.HBM) for array in operands))
    other = lax.ppermute(send, "grp", [(g, g ^ 1) for g in range(32)])
    chips = [[2 * chip + core for chip in range(16)] for core in range(2)]
    received = lax.all_to_all(keep + other, "grp", 0, 0, tiled=True, axis_index_groups=chips)
    middle = pl.pallas_call(
        middle_kernel,
        out_shape=jax.ShapeDtypeStruct((64, LANES), jnp.float32),
        in_specs=[vmem],
        out_specs=vmem,
        scratch_shapes=[pltpu.VMEM((256, LANES), jnp.float32)],
        name="middle",
    )(received)
    received = lax.all_to_all(middle.reshape(16, 4, LANES), "rep", 0, 0, tiled=True)
    return pl.pallas_call(
        last_kernel,
        out_shape=jax.ShapeDtypeStruct((7, 2, 2, 16), jnp.float32),
        in_specs=[vmem],
        out_specs=vmem,
        name="last",
    )(received)


def solution(mesh):
    return jax.shard_map(
        shards,
        mesh=mesh,
        in_specs=(
            P(None, None, ("grp", "rep"), None),
            P(("grp", "rep"), None, None, None),
            P(None, ("grp", "rep"), None, None),
            P(),
        ),
        out_specs=P("rep", None, None, "grp"),
        check_vma=False,
    )
```

```python
import functools

import jax
import jax.numpy as jnp
from jax import lax
from jax.experimental import pallas as pl
from jax.experimental.pallas import tpu as pltpu
from jax.sharding import PartitionSpec as P

LANES = 128


def halves(value):
    high = value.astype(jnp.bfloat16)
    low = (value - high.astype(jnp.float32)).astype(jnp.bfloat16)
    return high, low


def dot(left, right):
    return jnp.dot(left, right, preferred_element_type=jnp.float32)


def partial_kernel(
    place_of, amps_hbm, ints_hbm, cycle_hbm, sym_hbm, labels_hbm, keep_ref, send_ref,
    amps_ref, ints_ref, cycle_ref, sym_ref, sym_scalars, wide_ref, turned_ref, sems,
):
    tiles = 4
    occupied = 112
    columns = 16
    rows = 2 * columns * 8
    parts = 4
    depth = 4096 // parts
    pairs = [
        (labels_hbm, sym_scalars),
        (sym_hbm, sym_ref),
        (amps_hbm, amps_ref.at[pl.ds(0, 2 * occupied * tiles)]),
        (cycle_hbm, cycle_ref.at[pl.ds(0, 2 * occupied)]),
    ]
    for part in range(parts):
        at = pl.ds(part * depth, depth)
        pairs.append((ints_hbm.at[at], ints_ref.at[at]))
    copies = [pltpu.make_async_copy(source, target, sems.at[n]) for n, (source, target) in enumerate(pairs)]
    for copy in copies:
        copy.start()
    owner, core = place_of()
    for copy in copies[:4]:
        copy.wait()
    own_sym = sym_scalars[owner]
    amps_ref[pl.ds(2 * occupied * tiles, 8), :] = jnp.zeros((8, LANES), jnp.float32)
    chunks = []
    for tile in range(tiles):
        groups = [
            amps_ref[pl.ds((i * occupied + z * 7) * tiles + tile, 8, stride=tiles), :]
            for i in range(2)
            for z in range(columns)
        ]
        chunks.append(halves(jnp.concatenate(groups, axis=0)))
    left = jnp.concatenate(
        [
            jnp.concatenate([high for high, _ in chunks], axis=1),
            jnp.concatenate([low for _, low in chunks], axis=1),
        ],
        axis=0,
    )
    eighth = lax.broadcasted_iota(jnp.int32, (8, occupied), 0) == 7
    turned = []
    for a in range(2):
        groups = [
            jnp.where(eighth, 0.0, cycle_ref[pl.ds(z * 14 + a, 8, stride=2), :]) for z in range(columns)
        ]
        block = jnp.concatenate(groups, axis=0)
        block = jnp.concatenate([block, jnp.zeros((LANES, LANES - occupied), jnp.float32)], axis=1)
        turned_ref[a] = block.T
        turned += [turned_ref[a, pl.ds(z * 7, 8), :] for z in range(columns)]
    cycle_high, cycle_low = halves(jnp.concatenate(turned, axis=0))
    cycle_left = jnp.concatenate([cycle_high, cycle_low, cycle_high], axis=1)
    sym_columns = jnp.concatenate(
        [jnp.broadcast_to(sym_ref[tile : tile + 1, :], (LANES, LANES)).T for tile in range(tiles)], axis=0
    )
    for part in range(parts):
        copies[4 + part].wait()
        at = pl.ds(part * depth, depth)
        wide_ref[at, :] = ints_ref[at, :].astype(jnp.float32)
    for tile in range(tiles):
        label = jnp.bitwise_xor(sym_columns, sym_ref[tile : tile + 1, :])
        masked = []
        for a in range(2):
            block = wide_ref[pl.ds(tile * 2 + a, 512, stride=8), :]
            wanted = jnp.bitwise_xor(own_sym, sym_scalars[a])
            masked.append(jnp.where(label == wanted, block, 0.0).astype(jnp.bfloat16))
        both = dot(left, jnp.concatenate(masked, axis=1))
        ladder = both[:rows] + both[rows:]
        high, low = chunks[tile]
        right = jnp.concatenate(
            [
                jnp.concatenate([value[:LANES], value[LANES:]], axis=1)
                for value in (high, high, low)
            ],
            axis=0,
        )
        cycle = dot(cycle_left, right)
        blocks = []
        for half in range(2):
            for a in range(2):
                groups = []
                for z in range(8 * half, 8 * half + 8):
                    for i in range(2):
                        first, second = i * LANES, a * LANES
                        groups.append(
                            ladder[first + 8 * z : first + 8 * z + 8, second : second + LANES]
                            + cycle[second + 8 * z : second + 8 * z + 8, first : first + LANES]
                        )
                blocks.append(jnp.concatenate(groups, axis=0).T)
        for part in range(4):
            chip = tile * 4 + part
            for n, block in enumerate(blocks):
                zero = block[part * 32 : part * 32 + 16]
                one = block[part * 32 + 16 : part * 32 + 32]
                keep_ref[chip, 16 * n : 16 * n + 16, :] = jnp.where(core == 0, zero, one)
                send_ref[chip, 16 * n : 16 * n + 16, :] = jnp.where(core == 0, one, zero)


def shards(amplitudes, ladder_ints, cycle_ints, virt_sym):
    amps = amplitudes.reshape(896, LANES)
    ints = ladder_ints.reshape(512, 2, 4, LANES).transpose(0, 2, 1, 3).reshape(4096, LANES)
    cycle = cycle_ints.reshape(112, 112, 2).transpose(0, 2, 1).reshape(224, 112)

    def place_of():
        group = lax.axis_index("grp")
        return group * 16 + lax.axis_index("rep"), lax.rem(group, 2)

    hbm = pl.BlockSpec(memory_space=pltpu.HBM)
    vmem = pl.BlockSpec(memory_space=pltpu.VMEM)
    operands = (amps, ints, cycle, virt_sym.reshape(4, LANES), virt_sym)
    half = jax.ShapeDtypeStruct((16, 64, LANES), jnp.float32)
    keep, send = pl.pallas_call(
        functools.partial(partial_kernel, place_of),
        out_shape=(half, half),
        in_specs=[hbm] * 5,
        out_specs=(vmem, vmem),
        scratch_shapes=[
            pltpu.VMEM((904, LANES), jnp.float32),
            pltpu.VMEM((4096, LANES), jnp.bfloat16),
            pltpu.VMEM((232, 112), jnp.float32),
            pltpu.VMEM((4, LANES), jnp.int32),
            pltpu.SMEM((512,), jnp.int32),
            pltpu.VMEM((4096, LANES), jnp.float32),
            pltpu.VMEM((2, LANES, LANES), jnp.float32),
            pltpu.SemaphoreType.DMA((8,)),
        ],
        compiler_params=pltpu.CompilerParams(vmem_limit_bytes=32 * 1024 * 1024),
        name="partial",
    )(*(pltpu.with_memory_space_constraint(array, pltpu.HBM) for array in operands))
    other = lax.ppermute(send, "grp", [(g, g ^ 1) for g in range(32)])
    chips = [[2 * chip + core for chip in range(16)] for core in range(2)]
    received = lax.all_to_all(keep + other, "grp", 0, 0, tiled=True, axis_index_groups=chips)
    summed = received.sum(axis=0).reshape(2, 32, LANES).transpose(0, 2, 1).reshape(16, 4, LANES)
    received = lax.all_to_all(summed, "rep", 0, 0, tiled=True)
    return received.sum(axis=0).reshape(2, 8, 2, 16)[:, :7].transpose(1, 0, 2, 3)


def solution(mesh):
    return jax.shard_map(
        shards,
        mesh=mesh,
        in_specs=(
            P(None, None, ("grp", "rep"), None),
            P(("grp", "rep"), None, None, None),
            P(None, ("grp", "rep"), None, None),
            P(),
        ),
        out_specs=P("rep", None, None, "grp"),
        check_vma=False,
    )
```

```python
import functools

import jax
import jax.numpy as jnp
from jax import lax
from jax.experimental import pallas as pl
from jax.experimental.pallas import tpu as pltpu
from jax.sharding import PartitionSpec as P

LANES = 128
REP_ORDER = [(z + 8) % 16 for z in range(16)]
CHIP_ORDER = [(chip + 10) % 16 for chip in range(16)]


def halves(value):
    high = value.astype(jnp.bfloat16)
    low = (value - high.astype(jnp.float32)).astype(jnp.bfloat16)
    return high, low


def dot(left, right):
    return jnp.dot(left, right, preferred_element_type=jnp.float32)


def partial_kernel(
    place_of, amps_hbm, ints_hbm, cycle_hbm, sym_hbm, labels_hbm, keep_ref, send_ref,
    amps_ref, ints_ref, cycle_ref, sym_ref, sym_scalars, wide_ref, turned_ref, sems,
):
    tiles = 4
    occupied = 112
    columns = 16
    rows = 2 * columns * 8
    parts = 4
    depth = 4096 // parts
    pairs = [
        (labels_hbm, sym_scalars),
        (sym_hbm, sym_ref),
        (amps_hbm, amps_ref.at[pl.ds(0, 2 * occupied * tiles)]),
        (cycle_hbm, cycle_ref.at[pl.ds(0, 2 * occupied)]),
    ]
    for part in range(parts):
        at = pl.ds(part * depth, depth)
        pairs.append((ints_hbm.at[at], ints_ref.at[at]))
    copies = [pltpu.make_async_copy(source, target, sems.at[n]) for n, (source, target) in enumerate(pairs)]
    for copy in copies:
        copy.start()
    owner, core = place_of()
    for copy in copies[:4]:
        copy.wait()
    own_sym = sym_scalars[owner]
    amps_ref[pl.ds(2 * occupied * tiles, 8), :] = jnp.zeros((8, LANES), jnp.float32)
    chunks = []
    for tile in range(tiles):
        groups = [
            amps_ref[pl.ds((i * occupied + z * 7) * tiles + tile, 8, stride=tiles), :]
            for i in range(2)
            for z in range(columns)
        ]
        chunks.append(halves(jnp.concatenate(groups, axis=0)))
    left = jnp.concatenate(
        [
            jnp.concatenate([high for high, _ in chunks], axis=1),
            jnp.concatenate([low for _, low in chunks], axis=1),
        ],
        axis=0,
    )
    eighth = lax.broadcasted_iota(jnp.int32, (8, occupied), 0) == 7
    turned = []
    for a in range(2):
        groups = [
            jnp.where(eighth, 0.0, cycle_ref[pl.ds(z * 14 + a, 8, stride=2), :]) for z in range(columns)
        ]
        block = jnp.concatenate(groups, axis=0)
        block = jnp.concatenate([block, jnp.zeros((LANES, LANES - occupied), jnp.float32)], axis=1)
        turned_ref[a] = block.T
        turned += [turned_ref[a, pl.ds(z * 7, 8), :] for z in range(columns)]
    cycle_high, cycle_low = halves(jnp.concatenate(turned, axis=0))
    cycle_left = jnp.concatenate([cycle_high, cycle_low, cycle_high], axis=1)
    sym_columns = jnp.concatenate(
        [jnp.broadcast_to(sym_ref[tile : tile + 1, :], (LANES, LANES)).T for tile in range(tiles)], axis=0
    )
    for part in range(parts):
        copies[4 + part].wait()
        at = pl.ds(part * depth, depth)
        wide_ref[at, :] = ints_ref[at, :].astype(jnp.float32)
    for tile in range(tiles):
        label = jnp.bitwise_xor(sym_columns, sym_ref[tile : tile + 1, :])
        masked = []
        for a in range(2):
            block = wide_ref[pl.ds(tile * 2 + a, 512, stride=8), :]
            wanted = jnp.bitwise_xor(own_sym, sym_scalars[a])
            masked.append(jnp.where(label == wanted, block, 0.0).astype(jnp.bfloat16))
        both = dot(left, jnp.concatenate(masked, axis=1))
        ladder = both[:rows] + both[rows:]
        high, low = chunks[tile]
        right = jnp.concatenate(
            [
                jnp.concatenate([value[:LANES], value[LANES:]], axis=1)
                for value in (high, high, low)
            ],
            axis=0,
        )
        cycle = dot(cycle_left, right)
        blocks = []
        for half in range(2):
            for a in range(2):
                groups = []
                for z in REP_ORDER[8 * half : 8 * half + 8]:
                    for i in range(2):
                        first, second = i * LANES, a * LANES
                        groups.append(
                            ladder[first + 8 * z : first + 8 * z + 8, second : second + LANES]
                            + cycle[second + 8 * z : second + 8 * z + 8, first : first + LANES]
                        )
                blocks.append(jnp.concatenate(groups, axis=0).T)
        for part in range(4):
            chip = CHIP_ORDER.index(tile * 4 + part)
            for n, block in enumerate(blocks):
                zero = block[part * 32 : part * 32 + 16]
                one = block[part * 32 + 16 : part * 32 + 32]
                keep_ref[chip, 16 * n : 16 * n + 16, :] = jnp.where(core == 0, zero, one)
                send_ref[chip, 16 * n : 16 * n + 16, :] = jnp.where(core == 0, one, zero)


def shards(amplitudes, ladder_ints, cycle_ints, virt_sym):
    amps = amplitudes.reshape(896, LANES)
    ints = ladder_ints.reshape(512, 2, 4, LANES).transpose(0, 2, 1, 3).reshape(4096, LANES)
    cycle = cycle_ints.reshape(112, 112, 2).transpose(0, 2, 1).reshape(224, 112)

    def place_of():
        group = lax.axis_index("grp")
        return group * 16 + lax.axis_index("rep"), lax.rem(group, 2)

    hbm = pl.BlockSpec(memory_space=pltpu.HBM)
    vmem = pl.BlockSpec(memory_space=pltpu.VMEM)
    operands = (amps, ints, cycle, virt_sym.reshape(4, LANES), virt_sym)
    half = jax.ShapeDtypeStruct((16, 64, LANES), jnp.float32)
    keep, send = pl.pallas_call(
        functools.partial(partial_kernel, place_of),
        out_shape=(half, half),
        in_specs=[hbm] * 5,
        out_specs=(vmem, vmem),
        scratch_shapes=[
            pltpu.VMEM((904, LANES), jnp.float32),
            pltpu.VMEM((4096, LANES), jnp.bfloat16),
            pltpu.VMEM((232, 112), jnp.float32),
            pltpu.VMEM((4, LANES), jnp.int32),
            pltpu.SMEM((512,), jnp.int32),
            pltpu.VMEM((4096, LANES), jnp.float32),
            pltpu.VMEM((2, LANES, LANES), jnp.float32),
            pltpu.SemaphoreType.DMA((8,)),
        ],
        compiler_params=pltpu.CompilerParams(vmem_limit_bytes=32 * 1024 * 1024),
        name="partial",
    )(*(pltpu.with_memory_space_constraint(array, pltpu.HBM) for array in operands))
    other = lax.ppermute(send, "grp", [(g, g ^ 1) for g in range(32)])
    chips = [[2 * chip + core for chip in CHIP_ORDER] for core in range(2)]
    received = lax.all_to_all(keep + other, "grp", 0, 0, tiled=True, axis_index_groups=chips)
    summed = received.sum(axis=0).reshape(2, 32, LANES).transpose(0, 2, 1).reshape(16, 4, LANES)
    received = lax.all_to_all(summed, "rep", 0, 0, tiled=True, axis_index_groups=[REP_ORDER])
    return received.sum(axis=0).reshape(2, 8, 2, 16)[:, :7].transpose(1, 0, 2, 3)


def solution(mesh):
    return jax.shard_map(
        shards,
        mesh=mesh,
        in_specs=(
            P(None, None, ("grp", "rep"), None),
            P(("grp", "rep"), None, None, None),
            P(None, ("grp", "rep"), None, None),
            P(),
        ),
        out_specs=P("rep", None, None, "grp"),
        check_vma=False,
    )
```

```python
import functools

import jax
import jax.numpy as jnp
from jax import lax
from jax.experimental import pallas as pl
from jax.experimental.pallas import tpu as pltpu
from jax.sharding import PartitionSpec as P

LANES = 128
REP_ORDER = [(z + 8) % 16 for z in range(16)]
CHIP_ORDER = [(chip + 10) % 16 for chip in range(16)]


def halves(value):
    high = value.astype(jnp.bfloat16)
    low = (value - high.astype(jnp.float32)).astype(jnp.bfloat16)
    return high, low


def dot(left, right):
    return jnp.dot(left, right, preferred_element_type=jnp.float32)


def packed(firsts, seconds, at, lanes):
    pieces = [firsts[a][at + half : at + half + 8] for a in range(2) for half in (0, 8)]
    body = [seconds[0][at : at + 8], seconds[0][at + 8 : at + 16], seconds[1][at : at + 8]]
    last = seconds[1][at + 8 : at + 16]
    for piece in range(3):
        moved = pltpu.roll(last, 96 - 32 * piece, 1)
        pieces.append(jnp.where(lanes < 96, body[piece], moved))
    return pieces


def partial_kernel(
    place_of, amps_hbm, ints_hbm, cycle_hbm, sym_hbm, labels_hbm, keep_ref, send_ref,
    amps_ref, ints_ref, cycle_ref, sym_ref, sym_scalars, wide_ref, turned_ref, sems,
):
    tiles = 4
    occupied = 112
    columns = 16
    rows = 2 * occupied
    parts = 4
    depth = 4096 // parts
    pairs = [
        (amps_hbm, amps_ref),
        (cycle_hbm, cycle_ref),
        (labels_hbm, sym_scalars),
        (sym_hbm, sym_ref),
    ]
    for part in range(parts):
        at = pl.ds(part * depth, depth)
        pairs.append((ints_hbm.at[at], ints_ref.at[at]))
    copies = [pltpu.make_async_copy(source, target, sems.at[n]) for n, (source, target) in enumerate(pairs)]
    for copy in copies:
        copy.start()
    owner, core = place_of()
    for copy in copies[:4]:
        copy.wait()
    own_sym = sym_scalars[owner]
    starts = (7 * REP_ORDER[0], 7 * REP_ORDER[8])
    chunks = []
    for tile in range(tiles):
        groups = [
            amps_ref[pl.ds((i * occupied + start + jj) * tiles + tile, 8, stride=7 * tiles), :]
            for jj in range(7)
            for i in range(2)
            for start in starts
        ]
        chunks.append(halves(jnp.concatenate(groups, axis=0)))
    left = jnp.concatenate(
        [
            jnp.concatenate([high for high, _ in chunks], axis=1),
            jnp.concatenate([low for _, low in chunks], axis=1),
        ],
        axis=0,
    )
    pad = LANES - occupied
    turned = []
    for a in range(2):
        groups = [
            cycle_ref[pl.ds((start + jj) * 2 + a, 8, stride=14), :] for jj in range(7) for start in starts
        ]
        block = jnp.concatenate(groups + [jnp.zeros((pad, occupied), jnp.float32)], axis=0)
        block = jnp.concatenate([block, jnp.zeros((LANES, pad), jnp.float32)], axis=1)
        turned_ref[a] = block.T
        turned += [turned_ref[a, pl.ds(start + jj, 8, stride=7), :] for jj in range(7) for start in starts]
    cycle_high, cycle_low = halves(jnp.concatenate(turned, axis=0))
    cycle_left = jnp.concatenate([cycle_high, cycle_low, cycle_high], axis=1)
    zero_rows = jnp.zeros((pad, 2 * LANES), jnp.bfloat16)
    lanes = lax.broadcasted_iota(jnp.int32, (8, LANES), 1)
    sym_columns = jnp.concatenate(
        [jnp.broadcast_to(sym_ref[tile : tile + 1, :], (LANES, LANES)).T for tile in range(tiles)], axis=0
    )
    cycles = []
    for tile in range(tiles):
        high, low = chunks[tile]
        right = []
        for value in (high, high, low):
            sides = [
                jnp.concatenate([value[16 * (2 * jj + i) : 16 * (2 * jj + i) + 16] for jj in range(7)], axis=0)
                for i in range(2)
            ]
            right += [jnp.concatenate(sides, axis=1), zero_rows]
        right = jnp.concatenate(right, axis=0)
        cycles.append(dot(cycle_left, right))
    for part in range(parts):
        copies[4 + part].wait()
        at = pl.ds(part * depth, depth)
        wide_ref[at, :] = ints_ref[at, :].astype(jnp.float32)
    for tile in range(tiles):
        label = jnp.bitwise_xor(sym_columns, sym_ref[tile : tile + 1, :])
        masked = []
        for a in range(2):
            block = wide_ref[pl.ds(tile * 2 + a, 512, stride=8), :]
            wanted = jnp.bitwise_xor(own_sym, sym_scalars[a])
            masked.append(jnp.where(label == wanted, block, 0.0).astype(jnp.bfloat16))
        both = dot(left, jnp.concatenate(masked, axis=1))
        ladder = both[:rows] + both[rows:]
        firsts, seconds = [], []
        for a in range(2):
            groups = [
                cycles[tile][a * occupied + 16 * jj : a * occupied + 16 * jj + 16, i * LANES : (i + 1) * LANES]
                for jj in range(7)
                for i in range(2)
            ]
            total = ladder[:, a * LANES : (a + 1) * LANES] + jnp.concatenate(groups, axis=0)
            firsts.append(total[:LANES].T)
            rest = jnp.concatenate([total[LANES:], jnp.zeros((2 * LANES - rows, LANES), jnp.float32)], axis=0)
            seconds.append(rest.T)
        for part in range(4):
            chip = CHIP_ORDER.index(tile * 4 + part)
            zero, one = (packed(firsts, seconds, part * 32 + 16 * side, lanes) for side in range(2))
            for n in range(7):
                keep_ref[chip, 8 * n : 8 * n + 8, :] = jnp.where(core == 0, zero[n], one[n])
                send_ref[chip, 8 * n : 8 * n + 8, :] = jnp.where(core == 0, one[n], zero[n])


def shards(amplitudes, ladder_ints, cycle_ints, virt_sym):
    amps = amplitudes.reshape(896, LANES)
    ints = ladder_ints.reshape(512, 2, 4, LANES).transpose(0, 2, 1, 3).reshape(4096, LANES)
    cycle = cycle_ints.reshape(112, 112, 2).transpose(0, 2, 1).reshape(224, 112)

    def place_of():
        group = lax.axis_index("grp")
        return group * 16 + lax.axis_index("rep"), lax.rem(group, 2)

    hbm = pl.BlockSpec(memory_space=pltpu.HBM)
    vmem = pl.BlockSpec(memory_space=pltpu.VMEM)
    operands = (amps, ints, cycle, virt_sym.reshape(4, LANES), virt_sym)
    half = jax.ShapeDtypeStruct((16, 56, LANES), jnp.float32)
    keep, send = pl.pallas_call(
        functools.partial(partial_kernel, place_of),
        out_shape=(half, half),
        in_specs=[hbm] * 5,
        out_specs=(vmem, vmem),
        scratch_shapes=[
            pltpu.VMEM((896, LANES), jnp.float32),
            pltpu.VMEM((4096, LANES), jnp.bfloat16),
            pltpu.VMEM((224, 112), jnp.float32),
            pltpu.VMEM((4, LANES), jnp.int32),
            pltpu.SMEM((512,), jnp.int32),
            pltpu.VMEM((4096, LANES), jnp.float32),
            pltpu.VMEM((2, LANES, LANES), jnp.float32),
            pltpu.SemaphoreType.DMA((8,)),
        ],
        compiler_params=pltpu.CompilerParams(vmem_limit_bytes=32 * 1024 * 1024),
        name="partial",
    )(*(pltpu.with_memory_space_constraint(array, pltpu.HBM) for array in operands))
    other = lax.ppermute(send, "grp", [(g, g ^ 1) for g in range(32)])
    chips = [[2 * chip + core for chip in CHIP_ORDER] for core in range(2)]
    received = lax.all_to_all(keep + other, "grp", 0, 0, tiled=True, axis_index_groups=chips)
    summed = received.sum(axis=0).reshape(56, 8, 16).transpose(2, 1, 0)
    summed = jnp.pad(summed, ((0, 0), (0, 0), (0, 8))).reshape(16, 4, LANES)
    received = lax.all_to_all(summed, "rep", 0, 0, tiled=True, axis_index_groups=[REP_ORDER])
    block = received.sum(axis=0).reshape(8, 64)[:, :56]
    last = block[6:, 32:].reshape(2, 3, 8).transpose(1, 0, 2).reshape(6, 8)
    rest = jnp.concatenate([block[:6, 32:], last], axis=1)
    return jnp.concatenate([block[:, :32], rest], axis=0).reshape(7, 2, 2, 16)


def solution(mesh):
    return jax.shard_map(
        shards,
        mesh=mesh,
        in_specs=(
            P(None, None, ("grp", "rep"), None),
            P(("grp", "rep"), None, None, None),
            P(None, ("grp", "rep"), None, None),
            P(),
        ),
        out_specs=P("rep", None, None, "grp"),
        check_vma=False,
    )
```

```python
import functools

import jax
import jax.numpy as jnp
from jax import lax
from jax.experimental import pallas as pl
from jax.experimental.pallas import tpu as pltpu
from jax.sharding import PartitionSpec as P

LANES = 128
REP_ORDER = [(z + 8) % 16 for z in range(16)]
CHIP_ORDER = [(chip + 10) % 16 for chip in range(16)]


def halves(value):
    high = value.astype(jnp.bfloat16)
    low = (value - high.astype(jnp.float32)).astype(jnp.bfloat16)
    return high, low


def dot(left, right):
    return jnp.dot(left, right, preferred_element_type=jnp.float32)


def rolled(piece, groups):
    return piece if groups % 8 == 0 else pltpu.roll(piece, 16 * (groups % 8), 1)


def exchanged(pieces, lane_groups):
    turned = [rolled(pieces[s], s) for s in range(8)]
    picked = [turned[-n % 8] for n in range(8)]
    for step in (1, 2, 4):
        take = (lane_groups & step) != 0
        picked = [jnp.where(take, picked[(n - step) % 8], picked[n]) for n in range(8)]
    return [rolled(picked[n], -n) for n in range(8)]


def partial_kernel(
    place_of, amps_hbm, ints_hbm, cycle_hbm, sym_hbm, labels_hbm, keep_ref, send_ref,
    amps_ref, ints_ref, cycle_ref, sym_ref, sym_scalars, wide_ref, turned_ref, sems,
):
    tiles = 4
    occupied = 112
    rows = 2 * occupied
    parts = 2
    depth = 4096 // parts
    pairs = [
        (amps_hbm, amps_ref),
        (cycle_hbm, cycle_ref),
        (labels_hbm, sym_scalars),
        (sym_hbm, sym_ref),
    ]
    for part in range(parts):
        at = pl.ds(part * depth, depth)
        pairs.append((ints_hbm.at[at], ints_ref.at[at]))
    copies = [pltpu.make_async_copy(source, target, sems.at[n]) for n, (source, target) in enumerate(pairs)]
    for copy in copies:
        copy.start()
    owner, core = place_of()
    for copy in copies[:4]:
        copy.wait()
    own_sym = sym_scalars[owner]
    starts = (7 * REP_ORDER[0], 7 * REP_ORDER[8])
    chunks, rights = [], []
    for tile in range(tiles):
        groups = {
            (half, i, jj): amps_ref[pl.ds((i * occupied + start + jj) * tiles + tile, 8, stride=7 * tiles), :]
            for half, start in enumerate(starts)
            for i in range(2)
            for jj in range(7)
        }
        chunks.append(halves(jnp.concatenate(list(groups.values()), axis=0)))
        sides = [
            jnp.concatenate([groups[half, i, jj] for half in range(2) for jj in range(7)], axis=0) for i in range(2)
        ]
        rights.append(halves(jnp.concatenate(sides, axis=1)))
    left = jnp.concatenate(
        [
            jnp.concatenate([high for high, _ in chunks], axis=1),
            jnp.concatenate([low for _, low in chunks], axis=1),
        ],
        axis=0,
    )
    pad = LANES - occupied
    turned = []
    for a in range(2):
        groups = [
            cycle_ref[pl.ds((start + jj) * 2 + a, 8, stride=14), :] for start in starts for jj in range(7)
        ]
        block = jnp.concatenate(groups + [jnp.zeros((pad, occupied), jnp.float32)], axis=0)
        block = jnp.concatenate([block, jnp.zeros((LANES, pad), jnp.float32)], axis=1)
        turned_ref[a] = block.T
        turned += [turned_ref[a, pl.ds(start + jj, 8, stride=7), :] for start in starts for jj in range(7)]
    cycle_high, cycle_low = halves(jnp.concatenate(turned, axis=0))
    cycle_left = jnp.concatenate([cycle_high, cycle_low, cycle_high], axis=1)
    zero_rows = jnp.zeros((pad, 2 * LANES), jnp.bfloat16)
    lane_groups = lax.broadcasted_iota(jnp.int32, (8, LANES), 1) // 16
    sym_columns = jnp.concatenate(
        [jnp.broadcast_to(sym_ref[tile : tile + 1, :], (LANES, LANES)).T for tile in range(tiles)], axis=0
    )
    cycles = []
    for tile in range(tiles):
        high, low = rights[tile]
        right = jnp.concatenate([high, zero_rows, high, zero_rows, low, zero_rows], axis=0)
        cycles.append(dot(cycle_left, right))
    for part in range(parts):
        copies[4 + part].wait()
        at = pl.ds(part * depth, depth)
        wide_ref[at, :] = ints_ref[at, :].astype(jnp.float32)
    for tile in range(tiles):
        label = jnp.bitwise_xor(sym_columns, sym_ref[tile : tile + 1, :])
        masked = []
        for a in range(2):
            block = wide_ref[pl.ds(tile * 2 + a, 512, stride=8), :]
            wanted = jnp.bitwise_xor(own_sym, sym_scalars[a])
            masked.append(jnp.where(label == wanted, block, 0.0).astype(jnp.bfloat16))
        both = dot(left, jnp.concatenate(masked, axis=1))
        ladder = both[:rows] + both[rows:]
        cycle = cycles[tile]
        for jj in range(7):
            pieces = []
            for half in range(2):
                for i in range(2):
                    for a in range(2):
                        row, other = 8 * ((2 * half + i) * 7 + jj), 8 * ((2 * a + half) * 7 + jj)
                        pieces.append(
                            ladder[row : row + 8, a * LANES : (a + 1) * LANES]
                            + cycle[other : other + 8, i * LANES : (i + 1) * LANES]
                        )
            pieces = exchanged(pieces, lane_groups)
            for part in range(4):
                chip = CHIP_ORDER.index(tile * 4 + part)
                zero, one = pieces[2 * part], pieces[2 * part + 1]
                keep_ref[chip, 8 * jj : 8 * jj + 8, :] = jnp.where(core == 0, zero, one)
                send_ref[chip, 8 * jj : 8 * jj + 8, :] = jnp.where(core == 0, one, zero)


def shards(amplitudes, ladder_ints, cycle_ints, virt_sym):
    amps = amplitudes.reshape(896, LANES)
    ints = ladder_ints.reshape(512, 2, 4, LANES).transpose(0, 2, 1, 3).reshape(4096, LANES)
    cycle = cycle_ints.reshape(112, 112, 2).transpose(0, 2, 1).reshape(224, 112)

    def place_of():
        group = lax.axis_index("grp")
        return group * 16 + lax.axis_index("rep"), lax.rem(group, 2)

    hbm = pl.BlockSpec(memory_space=pltpu.HBM)
    vmem = pl.BlockSpec(memory_space=pltpu.VMEM)
    operands = (amps, ints, cycle, virt_sym.reshape(4, LANES), virt_sym)
    half = jax.ShapeDtypeStruct((16, 56, LANES), jnp.float32)
    keep, send = pl.pallas_call(
        functools.partial(partial_kernel, place_of),
        out_shape=(half, half),
        in_specs=[hbm] * 5,
        out_specs=(vmem, vmem),
        scratch_shapes=[
            pltpu.VMEM((896, LANES), jnp.float32),
            pltpu.VMEM((4096, LANES), jnp.bfloat16),
            pltpu.VMEM((224, 112), jnp.float32),
            pltpu.VMEM((4, LANES), jnp.int32),
            pltpu.SMEM((512,), jnp.int32),
            pltpu.VMEM((4096, LANES), jnp.float32),
            pltpu.VMEM((2, LANES, LANES), jnp.float32),
            pltpu.SemaphoreType.DMA((6,)),
        ],
        compiler_params=pltpu.CompilerParams(vmem_limit_bytes=32 * 1024 * 1024),
        name="partial",
    )(*(pltpu.with_memory_space_constraint(array, pltpu.HBM) for array in operands))
    other = lax.ppermute(send, "grp", [(g, g ^ 1) for g in range(32)])
    chips = [[2 * chip + core for chip in CHIP_ORDER] for core in range(2)]
    received = lax.all_to_all(keep + other, "grp", 0, 0, tiled=True, axis_index_groups=chips)
    summed = received.sum(axis=0).reshape(7, 8, 2, 64).transpose(2, 1, 0, 3).reshape(16, 448)
    summed = jnp.pad(summed, ((0, 0), (0, 64))).reshape(16, 4, LANES)
    received = lax.all_to_all(summed, "rep", 0, 0, tiled=True, axis_index_groups=[REP_ORDER])
    return received.sum(axis=0).reshape(512)[:448].reshape(7, 2, 2, 16)


def solution(mesh):
    return jax.shard_map(
        shards,
        mesh=mesh,
        in_specs=(
            P(None, None, ("grp", "rep"), None),
            P(("grp", "rep"), None, None, None),
            P(None, ("grp", "rep"), None, None),
            P(),
        ),
        out_specs=P("rep", None, None, "grp"),
        check_vma=False,
    )
```

```python
import functools

import jax
import jax.numpy as jnp
from jax import lax
from jax.experimental import pallas as pl
from jax.experimental.pallas import tpu as pltpu
from jax.sharding import PartitionSpec as P

LANES = 128
REP_ORDER = [(z + 8) % 16 for z in range(16)]
CHIP_ORDER = [(chip + 10) % 16 for chip in range(16)]


def halves(value):
    high = value.astype(jnp.bfloat16)
    low = (value - high.astype(jnp.float32)).astype(jnp.bfloat16)
    return high, low


def dot(left, right):
    return jnp.dot(left, right, preferred_element_type=jnp.float32)


def rolled(piece, groups):
    return piece if groups % 8 == 0 else pltpu.roll(piece, 16 * (groups % 8), 1)


def exchanged(pieces, lane_groups):
    turned = [rolled(pieces[s], s) for s in range(8)]
    picked = [turned[-n % 8] for n in range(8)]
    for step in (1, 2, 4):
        take = (lane_groups & step) != 0
        picked = [jnp.where(take, picked[(n - step) % 8], picked[n]) for n in range(8)]
    return [rolled(picked[n], -n) for n in range(8)]


TILES = 4
OCCUPIED = 112
STARTS = (7 * REP_ORDER[0], 7 * REP_ORDER[8])


def amp_groups(amps_ref, tile):
    return {
        (half, i, jj): amps_ref[pl.ds((i * OCCUPIED + start + jj) * TILES + tile, 8, stride=7 * TILES), :]
        for half, start in enumerate(STARTS)
        for i in range(2)
        for jj in range(7)
    }


def half_blocks(core, kept, left_ref, cycle_left_ref, wide_ref, amps_ref, columns_ref, labels_ref, out_ref):
    lane_groups = lax.broadcasted_iota(jnp.int32, (8, LANES), 1) // 16
    own_parity = (lane_groups & 1) == core
    shift = jnp.where(core == 0, 16, LANES - 16) if kept else jnp.where(core == 0, LANES - 16, 16)

    def merged(same, cross):
        mine = jnp.concatenate([own_parity] * (same.shape[0] // 8), axis=0)
        if kept:
            return jnp.where(mine, same, pltpu.roll(cross, shift, 1))
        return jnp.where(mine, pltpu.roll(same, shift, 1), cross)

    zero_rows = jnp.zeros((LANES - OCCUPIED, 2 * LANES), jnp.bfloat16)
    rows = 2 * OCCUPIED
    for pair in range(2):
        places = (2 * pair + core, 2 * pair + 1 - core)
        groups = [amp_groups(amps_ref, tile) for tile in places]
        sides = []
        for i in range(2):
            order = [(half, i, jj) for half in range(2) for jj in range(7)]
            sides.append(merged(*(jnp.concatenate([group[at] for at in order], axis=0) for group in groups)))
        high, low = halves(jnp.concatenate(sides, axis=1))
        right = jnp.concatenate([high, zero_rows, high, zero_rows, low, zero_rows], axis=0)
        cycle = dot(cycle_left_ref[...], right)
        labels = merged(*(labels_ref[pl.ds(pl.multiple_of(tile * 8, 8), 8), :] for tile in places))
        masked = []
        for a in range(2):
            block = merged(*(wide_ref[pl.ds(tile * 2 + a, 512, stride=8), :] for tile in places))
            wanted = jnp.bitwise_xor(labels, labels_ref[32 + 8 * a : 40 + 8 * a, :])[:1]
            masked.append(jnp.where(columns_ref[...] == wanted, block, 0.0).astype(jnp.bfloat16))
        both = dot(left_ref[...], jnp.concatenate(masked, axis=1))
        ladder = both[:rows] + both[rows:]
        for jj in range(7):
            pieces = []
            for half in range(2):
                for i in range(2):
                    for a in range(2):
                        row, other = 8 * ((2 * half + i) * 7 + jj), 8 * ((2 * a + half) * 7 + jj)
                        pieces.append(
                            ladder[row : row + 8, a * LANES : (a + 1) * LANES]
                            + cycle[other : other + 8, i * LANES : (i + 1) * LANES]
                        )
            for n, piece in enumerate(exchanged(pieces, lane_groups)):
                chip = CHIP_ORDER.index((2 * pair + n % 2) * 4 + n // 2)
                out_ref[chip, 8 * jj : 8 * jj + 8, :] = piece


def send_kernel(
    place_of, amps_hbm, ints_hbm, cycle_hbm, sym_hbm, scalars_hbm,
    send_ref, left_ref, cycle_left_ref, wide_ref, amps_ref, columns_ref, labels_ref,
    ints_ref, cycle_ref, sym_ref, sym_scalars, turned_ref, sems,
):
    parts = 2
    depth = 4096 // parts
    pairs = [
        (amps_hbm, amps_ref),
        (cycle_hbm, cycle_ref),
        (scalars_hbm, sym_scalars),
        (sym_hbm, sym_ref),
    ]
    for part in range(parts):
        at = pl.ds(part * depth, depth)
        pairs.append((ints_hbm.at[at], ints_ref.at[at]))
    copies = [pltpu.make_async_copy(source, target, sems.at[n]) for n, (source, target) in enumerate(pairs)]
    for copy in copies:
        copy.start()
    owner, core = place_of()
    for copy in copies[:4]:
        copy.wait()
    own_sym = sym_scalars[owner]
    for tile in range(TILES):
        row = sym_ref[tile : tile + 1, :]
        labels_ref[8 * tile : 8 * tile + 8, :] = jnp.broadcast_to(row, (8, LANES))
        columns_ref[LANES * tile : LANES * (tile + 1), :] = jnp.broadcast_to(row, (LANES, LANES)).T
    for a in range(2):
        wanted = jnp.bitwise_xor(own_sym, sym_scalars[a])
        labels_ref[32 + 8 * a : 40 + 8 * a, :] = jnp.full((8, LANES), wanted, jnp.int32)
    for tile in range(TILES):
        high, low = halves(jnp.concatenate(list(amp_groups(amps_ref, tile).values()), axis=0))
        left_ref[: 2 * OCCUPIED, LANES * tile : LANES * (tile + 1)] = high
        left_ref[2 * OCCUPIED :, LANES * tile : LANES * (tile + 1)] = low
    pad = LANES - OCCUPIED
    turned = []
    for a in range(2):
        groups = [
            cycle_ref[pl.ds((start + jj) * 2 + a, 8, stride=14), :] for start in STARTS for jj in range(7)
        ]
        block = jnp.concatenate(groups + [jnp.zeros((pad, OCCUPIED), jnp.float32)], axis=0)
        block = jnp.concatenate([block, jnp.zeros((LANES, pad), jnp.float32)], axis=1)
        turned_ref[a] = block.T
        turned += [turned_ref[a, pl.ds(start + jj, 8, stride=7), :] for start in STARTS for jj in range(7)]
    cycle_high, cycle_low = halves(jnp.concatenate(turned, axis=0))
    cycle_left_ref[...] = jnp.concatenate([cycle_high, cycle_low, cycle_high], axis=1)
    for part in range(parts):
        copies[4 + part].wait()
        at = pl.ds(part * depth, depth)
        wide_ref[at, :] = ints_ref[at, :].astype(jnp.float32)
    half_blocks(
        core, False, left_ref, cycle_left_ref, wide_ref, amps_ref, columns_ref, labels_ref, send_ref
    )


def keep_kernel(place_of, left_ref, cycle_left_ref, wide_ref, amps_ref, columns_ref, labels_ref, keep_ref):
    _, core = place_of()
    half_blocks(
        core, True, left_ref, cycle_left_ref, wide_ref, amps_ref, columns_ref, labels_ref, keep_ref
    )


def shards(amplitudes, ladder_ints, cycle_ints, virt_sym):
    amps = amplitudes.reshape(896, LANES)
    ints = ladder_ints.reshape(512, 2, 4, LANES).transpose(0, 2, 1, 3).reshape(4096, LANES)
    cycle = cycle_ints.reshape(112, 112, 2).transpose(0, 2, 1).reshape(224, 112)

    def place_of():
        group = lax.axis_index("grp")
        return group * 16 + lax.axis_index("rep"), lax.rem(group, 2)

    hbm = pl.BlockSpec(memory_space=pltpu.HBM)
    vmem = pl.BlockSpec(memory_space=pltpu.VMEM)
    operands = (amps, ints, cycle, virt_sym.reshape(4, LANES), virt_sym)
    half = jax.ShapeDtypeStruct((16, 56, LANES), jnp.float32)
    send, *rest = pl.pallas_call(
        functools.partial(send_kernel, place_of),
        out_shape=(
            half,
            jax.ShapeDtypeStruct((448, 512), jnp.bfloat16),
            jax.ShapeDtypeStruct((224, 3 * LANES), jnp.bfloat16),
            jax.ShapeDtypeStruct((4096, LANES), jnp.float32),
            jax.ShapeDtypeStruct((896, LANES), jnp.float32),
            jax.ShapeDtypeStruct((512, LANES), jnp.int32),
            jax.ShapeDtypeStruct((48, LANES), jnp.int32),
        ),
        in_specs=[hbm] * 5,
        out_specs=(vmem,) * 7,
        scratch_shapes=[
            pltpu.VMEM((4096, LANES), jnp.bfloat16),
            pltpu.VMEM((224, 112), jnp.float32),
            pltpu.VMEM((4, LANES), jnp.int32),
            pltpu.SMEM((512,), jnp.int32),
            pltpu.VMEM((2, LANES, LANES), jnp.float32),
            pltpu.SemaphoreType.DMA((6,)),
        ],
        compiler_params=pltpu.CompilerParams(vmem_limit_bytes=32 * 1024 * 1024),
        name="send",
    )(*(pltpu.with_memory_space_constraint(array, pltpu.HBM) for array in operands))
    other = lax.ppermute(send, "grp", [(g, g ^ 1) for g in range(32)])
    keep = pl.pallas_call(
        functools.partial(keep_kernel, place_of),
        out_shape=half,
        in_specs=[vmem] * 6,
        out_specs=vmem,
        compiler_params=pltpu.CompilerParams(vmem_limit_bytes=16 * 1024 * 1024),
        cost_estimate=pl.CostEstimate(flops=4 * 10**8, bytes_accessed=3 * 10**6, transcendentals=0),
        name="keep",
    )(*rest)
    chips = [[2 * chip + core for chip in CHIP_ORDER] for core in range(2)]
    received = lax.all_to_all(keep + other, "grp", 0, 0, tiled=True, axis_index_groups=chips)
    summed = received.sum(axis=0).reshape(7, 8, 2, 64).transpose(2, 1, 0, 3).reshape(16, 448)
    summed = jnp.pad(summed, ((0, 0), (0, 64))).reshape(16, 4, LANES)
    received = lax.all_to_all(summed, "rep", 0, 0, tiled=True, axis_index_groups=[REP_ORDER])
    return received.sum(axis=0).reshape(512)[:448].reshape(7, 2, 2, 16)


def solution(mesh):
    return jax.shard_map(
        shards,
        mesh=mesh,
        in_specs=(
            P(None, None, ("grp", "rep"), None),
            P(("grp", "rep"), None, None, None),
            P(None, ("grp", "rep"), None, None),
            P(),
        ),
        out_specs=P("rep", None, None, "grp"),
        check_vma=False,
    )
```

```python
import functools

import jax
import jax.numpy as jnp
from jax import lax
from jax.experimental import pallas as pl
from jax.experimental.pallas import tpu as pltpu
from jax.sharding import PartitionSpec as P

LANES = 128
REP_ORDER = [(z + 8) % 16 for z in range(16)]
CHIP_ORDER = [(chip + 10) % 16 for chip in range(16)]


def halves(value):
    high = value.astype(jnp.bfloat16)
    low = (value - high.astype(jnp.float32)).astype(jnp.bfloat16)
    return high, low


def dot(left, right):
    return jnp.dot(left, right, preferred_element_type=jnp.float32)


def rolled(piece, groups):
    return piece if groups % 8 == 0 else pltpu.roll(piece, 16 * (groups % 8), 1)


def exchanged(pieces, lane_groups):
    turned = [rolled(pieces[s], s) for s in range(8)]
    picked = [turned[-n % 8] for n in range(8)]
    for step in (1, 2, 4):
        take = (lane_groups & step) != 0
        picked = [jnp.where(take, picked[(n - step) % 8], picked[n]) for n in range(8)]
    return [rolled(picked[n], -n) for n in range(8)]


TILES = 4
OCCUPIED = 112
STARTS = (7 * REP_ORDER[0], 7 * REP_ORDER[8])


def amp_groups(amps_ref, tile):
    return {
        (half, i, jj): amps_ref[pl.ds((i * OCCUPIED + start + jj) * TILES + tile, 8, stride=7 * TILES), :]
        for half, start in enumerate(STARTS)
        for i in range(2)
        for jj in range(7)
    }


def half_blocks(core, kept, left_ref, cycle_left_ref, wide_ref, amps_ref, columns_ref, labels_ref, out_ref):
    lane_groups = lax.broadcasted_iota(jnp.int32, (8, LANES), 1) // 16
    own_parity = (lane_groups & 1) == core
    shift = jnp.where(core == 0, 16, LANES - 16) if kept else jnp.where(core == 0, LANES - 16, 16)

    def merged(same, cross):
        mine = jnp.concatenate([own_parity] * (same.shape[0] // 8), axis=0)
        if kept:
            return jnp.where(mine, same, pltpu.roll(cross, shift, 1))
        return jnp.where(mine, pltpu.roll(same, shift, 1), cross)

    zero_rows = jnp.zeros((LANES - OCCUPIED, 2 * LANES), jnp.bfloat16)
    rows = 2 * OCCUPIED
    for pair in range(2):
        places = (2 * pair + core, 2 * pair + 1 - core)
        groups = [amp_groups(amps_ref, tile) for tile in places]
        sides = []
        for i in range(2):
            order = [(half, i, jj) for half in range(2) for jj in range(7)]
            sides.append(merged(*(jnp.concatenate([group[at] for at in order], axis=0) for group in groups)))
        high, low = halves(jnp.concatenate(sides, axis=1))
        right = jnp.concatenate([high, zero_rows, high, zero_rows, low, zero_rows], axis=0)
        cycle = dot(cycle_left_ref[...], right)
        labels = merged(*(labels_ref[pl.ds(pl.multiple_of(tile * 8, 8), 8), :] for tile in places))
        masked = []
        for a in range(2):
            block = merged(*(wide_ref[pl.ds(tile * 2 + a, 512, stride=8), :] for tile in places))
            wanted = jnp.bitwise_xor(labels, labels_ref[32 + 8 * a : 40 + 8 * a, :])[:1]
            masked.append(jnp.where(columns_ref[...] == wanted, block, 0.0).astype(jnp.bfloat16))
        both = dot(left_ref[...], jnp.concatenate(masked, axis=1))
        ladder = both[:rows] + both[rows:]
        for jj in range(7):
            pieces = []
            for half in range(2):
                for i in range(2):
                    for a in range(2):
                        row, other = 8 * ((2 * half + i) * 7 + jj), 8 * ((2 * a + half) * 7 + jj)
                        pieces.append(
                            ladder[row : row + 8, a * LANES : (a + 1) * LANES]
                            + cycle[other : other + 8, i * LANES : (i + 1) * LANES]
                        )
            for n, piece in enumerate(exchanged(pieces, lane_groups)):
                chip = CHIP_ORDER.index((2 * pair + n % 2) * 4 + n // 2)
                out_ref[chip, 8 * jj : 8 * jj + 8, :] = piece


def send_kernel(
    place_of, amps_hbm, ints_hbm, cycle_hbm, sym_hbm, scalars_hbm,
    send_ref, left_ref, cycle_left_ref, wide_ref, amps_ref, columns_ref, labels_ref,
    ints_ref, cycle_ref, sym_ref, sym_scalars, turned_ref, sems,
):
    parts = 1
    depth = 4096 // parts
    pairs = [
        (amps_hbm, amps_ref),
        (cycle_hbm, cycle_ref),
        (scalars_hbm, sym_scalars),
        (sym_hbm, sym_ref),
    ]
    for part in range(parts):
        at = pl.ds(part * depth, depth)
        pairs.append((ints_hbm.at[at], ints_ref.at[at]))
    copies = [pltpu.make_async_copy(source, target, sems.at[n]) for n, (source, target) in enumerate(pairs)]
    for copy in copies:
        copy.start()
    owner, core = place_of()
    for copy in copies[:4]:
        copy.wait()
    own_sym = sym_scalars[owner]
    for tile in range(TILES):
        row = sym_ref[tile : tile + 1, :]
        labels_ref[8 * tile : 8 * tile + 8, :] = jnp.broadcast_to(row, (8, LANES))
        columns_ref[LANES * tile : LANES * (tile + 1), :] = jnp.broadcast_to(row, (LANES, LANES)).T
    for a in range(2):
        wanted = jnp.bitwise_xor(own_sym, sym_scalars[a])
        labels_ref[32 + 8 * a : 40 + 8 * a, :] = jnp.full((8, LANES), wanted, jnp.int32)
    for tile in range(TILES):
        high, low = halves(jnp.concatenate(list(amp_groups(amps_ref, tile).values()), axis=0))
        left_ref[: 2 * OCCUPIED, LANES * tile : LANES * (tile + 1)] = high
        left_ref[2 * OCCUPIED :, LANES * tile : LANES * (tile + 1)] = low
    pad = LANES - OCCUPIED
    turned = []
    for a in range(2):
        groups = [
            cycle_ref[pl.ds((start + jj) * 2 + a, 8, stride=14), :] for start in STARTS for jj in range(7)
        ]
        block = jnp.concatenate(groups + [jnp.zeros((pad, OCCUPIED), jnp.float32)], axis=0)
        block = jnp.concatenate([block, jnp.zeros((LANES, pad), jnp.float32)], axis=1)
        turned_ref[a] = block.T
        turned += [turned_ref[a, pl.ds(start + jj, 8, stride=7), :] for start in STARTS for jj in range(7)]
    cycle_high, cycle_low = halves(jnp.concatenate(turned, axis=0))
    cycle_left_ref[...] = jnp.concatenate([cycle_high, cycle_low, cycle_high], axis=1)
    for part in range(parts):
        copies[4 + part].wait()
        at = pl.ds(part * depth, depth)
        wide_ref[at, :] = ints_ref[at, :].astype(jnp.float32)
    half_blocks(
        core, False, left_ref, cycle_left_ref, wide_ref, amps_ref, columns_ref, labels_ref, send_ref
    )


def keep_kernel(place_of, left_ref, cycle_left_ref, wide_ref, amps_ref, columns_ref, labels_ref, keep_ref):
    _, core = place_of()
    half_blocks(
        core, True, left_ref, cycle_left_ref, wide_ref, amps_ref, columns_ref, labels_ref, keep_ref
    )


def shards(amplitudes, ladder_ints, cycle_ints, virt_sym):
    amps = amplitudes.reshape(896, LANES)
    ints = ladder_ints.reshape(512, 2, 4, LANES).transpose(0, 2, 1, 3).reshape(4096, LANES)
    cycle = cycle_ints.reshape(112, 112, 2).transpose(0, 2, 1).reshape(224, 112)

    def place_of():
        group = lax.axis_index("grp")
        return group * 16 + lax.axis_index("rep"), lax.rem(group, 2)

    hbm = pl.BlockSpec(memory_space=pltpu.HBM)
    vmem = pl.BlockSpec(memory_space=pltpu.VMEM)
    operands = (amps, ints, cycle, virt_sym.reshape(4, LANES), virt_sym)
    half = jax.ShapeDtypeStruct((16, 56, LANES), jnp.float32)
    send, *rest = pl.pallas_call(
        functools.partial(send_kernel, place_of),
        out_shape=(
            half,
            jax.ShapeDtypeStruct((448, 512), jnp.bfloat16),
            jax.ShapeDtypeStruct((224, 3 * LANES), jnp.bfloat16),
            jax.ShapeDtypeStruct((4096, LANES), jnp.float32),
            jax.ShapeDtypeStruct((896, LANES), jnp.float32),
            jax.ShapeDtypeStruct((512, LANES), jnp.int32),
            jax.ShapeDtypeStruct((48, LANES), jnp.int32),
        ),
        in_specs=[hbm] * 5,
        out_specs=(vmem,) * 7,
        scratch_shapes=[
            pltpu.VMEM((4096, LANES), jnp.bfloat16),
            pltpu.VMEM((224, 112), jnp.float32),
            pltpu.VMEM((4, LANES), jnp.int32),
            pltpu.SMEM((512,), jnp.int32),
            pltpu.VMEM((2, LANES, LANES), jnp.float32),
            pltpu.SemaphoreType.DMA((5,)),
        ],
        compiler_params=pltpu.CompilerParams(vmem_limit_bytes=32 * 1024 * 1024),
        name="send",
    )(*(pltpu.with_memory_space_constraint(array, pltpu.HBM) for array in operands))
    other = lax.ppermute(send, "grp", [(g, g ^ 1) for g in range(32)])
    keep = pl.pallas_call(
        functools.partial(keep_kernel, place_of),
        out_shape=half,
        in_specs=[vmem] * 6,
        out_specs=vmem,
        compiler_params=pltpu.CompilerParams(vmem_limit_bytes=16 * 1024 * 1024),
        cost_estimate=pl.CostEstimate(flops=4 * 10**8, bytes_accessed=3 * 10**6, transcendentals=0),
        name="keep",
    )(*rest)
    chips = [[2 * chip + core for chip in CHIP_ORDER] for core in range(2)]
    received = lax.all_to_all(keep + other, "grp", 0, 0, tiled=True, axis_index_groups=chips)
    summed = received.sum(axis=0).reshape(7, 8, 2, 64).transpose(2, 1, 0, 3).reshape(16, 448)
    summed = jnp.pad(summed, ((0, 0), (0, 64))).reshape(16, 4, LANES)
    received = lax.all_to_all(summed, "rep", 0, 0, tiled=True, axis_index_groups=[REP_ORDER])
    return received.sum(axis=0).reshape(512)[:448].reshape(7, 2, 2, 16)


def solution(mesh):
    return jax.shard_map(
        shards,
        mesh=mesh,
        in_specs=(
            P(None, None, ("grp", "rep"), None),
            P(("grp", "rep"), None, None, None),
            P(None, ("grp", "rep"), None, None),
            P(),
        ),
        out_specs=P("rep", None, None, "grp"),
        check_vma=False,
    )
```

```python
import functools

import jax
import jax.numpy as jnp
from jax import lax
from jax.experimental import pallas as pl
from jax.experimental.pallas import tpu as pltpu
from jax.sharding import PartitionSpec as P

LANES = 128
REP_ORDER = [(z + 8) % 16 for z in range(16)]
FIRST_CHIPS = (10, 14)


def halves(value):
    high = value.astype(jnp.bfloat16)
    low = (value - high.astype(jnp.float32)).astype(jnp.bfloat16)
    return high, low


def dot(left, right):
    return jnp.dot(left, right, preferred_element_type=jnp.float32)


def rolled(piece, groups):
    return piece if groups % 8 == 0 else pltpu.roll(piece, 16 * (groups % 8), 1)


def exchanged(pieces, lane_groups):
    turned = [rolled(pieces[s], s) for s in range(8)]
    picked = [turned[-n % 8] for n in range(8)]
    for step in (1, 2, 4):
        take = (lane_groups & step) != 0
        picked = [jnp.where(take, picked[(n - step) % 8], picked[n]) for n in range(8)]
    return [rolled(picked[n], -n) for n in range(8)]


TILES = 4
OCCUPIED = 112
STARTS = (7 * REP_ORDER[0], 7 * REP_ORDER[8])


def amp_groups(amps_ref, tile):
    return {
        (half, i, jj): amps_ref[pl.ds((i * OCCUPIED + start + jj) * TILES + tile, 8, stride=7 * TILES), :]
        for half, start in enumerate(STARTS)
        for i in range(2)
        for jj in range(7)
    }


def half_blocks(core, kept, left_ref, cycle_left_ref, wide_ref, amps_ref, columns_ref, labels_ref, out_ref):
    lane_groups = lax.broadcasted_iota(jnp.int32, (8, LANES), 1) // 16
    own_parity = (lane_groups & 1) == core
    shift = jnp.where(core == 0, 16, LANES - 16) if kept else jnp.where(core == 0, LANES - 16, 16)

    def merged(same, cross):
        mine = jnp.concatenate([own_parity] * (same.shape[0] // 8), axis=0)
        if kept:
            return jnp.where(mine, same, pltpu.roll(cross, shift, 1))
        return jnp.where(mine, pltpu.roll(same, shift, 1), cross)

    first_chip = jnp.where((core == 0) == kept, *FIRST_CHIPS)
    zero_rows = jnp.zeros((LANES - OCCUPIED, 2 * LANES), jnp.bfloat16)
    rows = 2 * OCCUPIED
    for pair in range(2):
        places = (2 * pair + core, 2 * pair + 1 - core)
        groups = [amp_groups(amps_ref, tile) for tile in places]
        sides = []
        for i in range(2):
            order = [(half, i, jj) for half in range(2) for jj in range(7)]
            sides.append(merged(*(jnp.concatenate([group[at] for at in order], axis=0) for group in groups)))
        high, low = halves(jnp.concatenate(sides, axis=1))
        right = jnp.concatenate([high, zero_rows, high, zero_rows, low, zero_rows], axis=0)
        cycle = dot(cycle_left_ref[...], right)
        labels = merged(*(labels_ref[pl.ds(pl.multiple_of(tile * 8, 8), 8), :] for tile in places))
        masked = []
        for a in range(2):
            block = merged(*(wide_ref[pl.ds(tile * 2 + a, 512, stride=8), :] for tile in places))
            wanted = jnp.bitwise_xor(labels, labels_ref[32 + 8 * a : 40 + 8 * a, :])[:1]
            masked.append(jnp.where(columns_ref[...] == wanted, block, 0.0).astype(jnp.bfloat16))
        both = dot(left_ref[...], jnp.concatenate(masked, axis=1))
        ladder = both[:rows] + both[rows:]
        for jj in range(7):
            pieces = []
            for half in range(2):
                for i in range(2):
                    for a in range(2):
                        row, other = 8 * ((2 * half + i) * 7 + jj), 8 * ((2 * a + half) * 7 + jj)
                        pieces.append(
                            ladder[row : row + 8, a * LANES : (a + 1) * LANES]
                            + cycle[other : other + 8, i * LANES : (i + 1) * LANES]
                        )
            for n, piece in enumerate(exchanged(pieces, lane_groups)):
                chip = lax.rem((2 * pair + n % 2) * 4 + n // 2 + 16 - first_chip, 16)
                out_ref[chip, 8 * jj : 8 * jj + 8, :] = piece


def send_kernel(
    place_of, amps_hbm, ints_hbm, cycle_hbm, sym_hbm, scalars_hbm,
    send_ref, left_ref, cycle_left_ref, wide_ref, amps_ref, columns_ref, labels_ref,
    ints_ref, cycle_ref, sym_ref, sym_scalars, turned_ref, sems,
):
    parts = 2
    depth = 4096 // parts
    pairs = [
        (amps_hbm, amps_ref),
        (cycle_hbm, cycle_ref),
        (scalars_hbm, sym_scalars),
        (sym_hbm, sym_ref),
    ]
    for part in range(parts):
        at = pl.ds(part * depth, depth)
        pairs.append((ints_hbm.at[at], ints_ref.at[at]))
    copies = [pltpu.make_async_copy(source, target, sems.at[n]) for n, (source, target) in enumerate(pairs)]
    for copy in copies:
        copy.start()
    owner, core = place_of()
    for copy in copies[:4]:
        copy.wait()
    own_sym = sym_scalars[owner]
    for tile in range(TILES):
        row = sym_ref[tile : tile + 1, :]
        labels_ref[8 * tile : 8 * tile + 8, :] = jnp.broadcast_to(row, (8, LANES))
        columns_ref[LANES * tile : LANES * (tile + 1), :] = jnp.broadcast_to(row, (LANES, LANES)).T
    for a in range(2):
        wanted = jnp.bitwise_xor(own_sym, sym_scalars[a])
        labels_ref[32 + 8 * a : 40 + 8 * a, :] = jnp.full((8, LANES), wanted, jnp.int32)
    for tile in range(TILES):
        high, low = halves(jnp.concatenate(list(amp_groups(amps_ref, tile).values()), axis=0))
        left_ref[: 2 * OCCUPIED, LANES * tile : LANES * (tile + 1)] = high
        left_ref[2 * OCCUPIED :, LANES * tile : LANES * (tile + 1)] = low
    pad = LANES - OCCUPIED
    turned = []
    for a in range(2):
        groups = [
            cycle_ref[pl.ds((start + jj) * 2 + a, 8, stride=14), :] for start in STARTS for jj in range(7)
        ]
        block = jnp.concatenate(groups + [jnp.zeros((pad, OCCUPIED), jnp.float32)], axis=0)
        block = jnp.concatenate([block, jnp.zeros((LANES, pad), jnp.float32)], axis=1)
        turned_ref[a] = block.T
        turned += [turned_ref[a, pl.ds(start + jj, 8, stride=7), :] for start in STARTS for jj in range(7)]
    cycle_high, cycle_low = halves(jnp.concatenate(turned, axis=0))
    cycle_left_ref[...] = jnp.concatenate([cycle_high, cycle_low, cycle_high], axis=1)
    for part in range(parts):
        copies[4 + part].wait()
        at = pl.ds(part * depth, depth)
        wide_ref[at, :] = ints_ref[at, :].astype(jnp.float32)
    half_blocks(
        core, False, left_ref, cycle_left_ref, wide_ref, amps_ref, columns_ref, labels_ref, send_ref
    )


def keep_kernel(place_of, left_ref, cycle_left_ref, wide_ref, amps_ref, columns_ref, labels_ref, keep_ref):
    _, core = place_of()
    half_blocks(
        core, True, left_ref, cycle_left_ref, wide_ref, amps_ref, columns_ref, labels_ref, keep_ref
    )


def shards(amplitudes, ladder_ints, cycle_ints, virt_sym):
    amps = amplitudes.reshape(896, LANES)
    ints = ladder_ints.reshape(512, 2, 4, LANES).transpose(0, 2, 1, 3).reshape(4096, LANES)
    cycle = cycle_ints.reshape(112, 112, 2).transpose(0, 2, 1).reshape(224, 112)

    def place_of():
        group = lax.axis_index("grp")
        return group * 16 + lax.axis_index("rep"), lax.rem(group, 2)

    hbm = pl.BlockSpec(memory_space=pltpu.HBM)
    vmem = pl.BlockSpec(memory_space=pltpu.VMEM)
    operands = (amps, ints, cycle, virt_sym.reshape(4, LANES), virt_sym)
    half = jax.ShapeDtypeStruct((16, 56, LANES), jnp.float32)
    send, *rest = pl.pallas_call(
        functools.partial(send_kernel, place_of),
        out_shape=(
            half,
            jax.ShapeDtypeStruct((448, 512), jnp.bfloat16),
            jax.ShapeDtypeStruct((224, 3 * LANES), jnp.bfloat16),
            jax.ShapeDtypeStruct((4096, LANES), jnp.float32),
            jax.ShapeDtypeStruct((896, LANES), jnp.float32),
            jax.ShapeDtypeStruct((512, LANES), jnp.int32),
            jax.ShapeDtypeStruct((48, LANES), jnp.int32),
        ),
        in_specs=[hbm] * 5,
        out_specs=(vmem,) * 7,
        scratch_shapes=[
            pltpu.VMEM((4096, LANES), jnp.bfloat16),
            pltpu.VMEM((224, 112), jnp.float32),
            pltpu.VMEM((4, LANES), jnp.int32),
            pltpu.SMEM((512,), jnp.int32),
            pltpu.VMEM((2, LANES, LANES), jnp.float32),
            pltpu.SemaphoreType.DMA((6,)),
        ],
        compiler_params=pltpu.CompilerParams(vmem_limit_bytes=32 * 1024 * 1024),
        name="send",
    )(*(pltpu.with_memory_space_constraint(array, pltpu.HBM) for array in operands))
    other = lax.ppermute(send, "grp", [(g, g ^ 1) for g in range(32)])
    keep = pl.pallas_call(
        functools.partial(keep_kernel, place_of),
        out_shape=half,
        in_specs=[vmem] * 6,
        out_specs=vmem,
        compiler_params=pltpu.CompilerParams(vmem_limit_bytes=16 * 1024 * 1024),
        cost_estimate=pl.CostEstimate(flops=4 * 10**8, bytes_accessed=3 * 10**6, transcendentals=0),
        name="keep",
    )(*rest)
    chips = [[2 * ((first + n) % 16) + core for n in range(16)] for core, first in enumerate(FIRST_CHIPS)]
    received = lax.all_to_all(keep + other, "grp", 0, 0, tiled=True, axis_index_groups=chips)
    summed = received.sum(axis=0).reshape(7, 8, 2, 64).transpose(2, 1, 0, 3).reshape(16, 448)
    summed = jnp.pad(summed, ((0, 0), (0, 64))).reshape(16, 4, LANES)
    received = lax.all_to_all(summed, "rep", 0, 0, tiled=True, axis_index_groups=[REP_ORDER])
    return received.sum(axis=0).reshape(512)[:448].reshape(7, 2, 2, 16)


def solution(mesh):
    return jax.shard_map(
        shards,
        mesh=mesh,
        in_specs=(
            P(None, None, ("grp", "rep"), None),
            P(("grp", "rep"), None, None, None),
            P(None, ("grp", "rep"), None, None),
            P(),
        ),
        out_specs=P("rep", None, None, "grp"),
        check_vma=False,
    )
```
